128 devices in a mesh: sub: 32 (over y, x, core), blk: 4 (over z).
Axes of the slice: x: 4, y: 4, z: 4, core: 2. Of those that a mesh axis runs over, the one named last changes fastest.
Arguments:
- coupling_blocks: float32 [256, 16, 9, 128, 128], P(('sub', 'blk')), may hold values from -0.12053519 to 1.3637
- block_inverse: float32 [256, 16, 128, 128], P(('sub', 'blk')), may hold values from -0.044194174 to 1.5, as said below
- coupling_pattern: int32 [256, 16, 9], P(('sub', 'blk')), may hold values 0 or 1
- link_blocks: int32 [256, 8], P(('sub', 'blk')), may hold values from 4 to 63, as said below
- interface_panel: float32 [8192, 512], P('sub', 'blk'), may hold values from -0.5 to 1.04, as said below
Outputs:
- panel_factor: float32 [8192, 512], P('sub', 'blk')
The draws below stay inside these ranges and needn't reach their ends.
Inputs may be any that keep to these rules, and one draw needn't show every extreme that they name: `block_inverse`: every block is symmetric. `link_blocks`: each row names 8 different interface blocks, none of the panel's first 4. `interface_panel`: the first 512 rows are symmetric.
All inputs are finite; a program needn't handle non-finite values. No bound on the sum of `coupling_pattern` on one device may be relied on, other than what follows from the above.
Results may differ from the reference program's by a relative error of at most 0.000075.
Values sent between devices are 32-bit elements; how exact they have to be, the bound alone decides.
A program may use at most 128 MiB of HBM per device.

```python
import jax
import jax.numpy as jnp
from jax import lax

BLK = 128
NI = 8192
LINKS = 8
CELLS = 16
SUB_DEV = 2
PBLK = 4
PW = 512
NB_I = 64
NSUBDOM = 256


def draw_coupling_blocks(key, part):
    key = jax.random.fold_in(key, 11)
    first_key, second_key = jax.random.split(key, 2)
    tile_shape = (NSUBDOM, CELLS, LINKS + 1, BLK, BLK)
    diagonal = jax.random.uniform(first_key, tile_shape[:-1] + (1,), jnp.float32, 1.0, 1.5)
    spread = jax.random.uniform(second_key, tile_shape, jnp.float32, -1.0, 1.0)
    identity = jnp.eye(BLK, dtype=jnp.float32)
    coupling = identity * diagonal + (1.0 - identity) * spread * (1.5 / BLK ** 0.5)
    weak_scale = (25.0 * CELLS * (NSUBDOM // PBLK)) ** (-0.5)
    strong_scale = 1.0 / (11.0 * CELLS * weak_scale)
    scales = jnp.where(jnp.arange(LINKS + 1) == 0, weak_scale, strong_scale).astype(jnp.float32)
    return coupling * scales[None, None, :, None, None]


def draw_block_inverse(key, part):
    key = jax.random.fold_in(key, 23)
    first_key, second_key = jax.random.split(key, 2)
    tile_shape = (NSUBDOM, CELLS, BLK, BLK)
    diagonal = jax.random.uniform(first_key, tile_shape[:-1] + (1,), jnp.float32, 1.0, 1.5)
    spread = jax.random.uniform(second_key, tile_shape, jnp.float32, -1.0, 1.0)
    symmetric = 0.5 * (spread + jnp.swapaxes(spread, -1, -2))
    identity = jnp.eye(BLK, dtype=jnp.float32)
    return identity * diagonal + (1.0 - identity) * symmetric * (0.5 / BLK ** 0.5)


def draw_link_blocks(key, part):
    key = jax.random.fold_in(key, 37)
    scores = jax.random.randint(key, (NSUBDOM, NB_I - PBLK), 0, 1 << 20)
    scores = scores * NB_I + jnp.arange(NB_I - PBLK, dtype=jnp.int32)[None, :]
    order = jnp.argsort(scores, axis=1, stable=True)
    return (order[:, :LINKS] + PBLK).astype(jnp.int32)


def draw_interface_panel(key, part):
    key = jax.random.fold_in(key, 53)
    upper_key, lower_key, diag_key = jax.random.split(key, 3)
    upper = jax.random.uniform(upper_key, (PW, PW), jnp.float32, -1.0, 1.0)
    diagonal = jax.random.uniform(diag_key, (PW,), jnp.float32, 0.96, 1.04)
    lower = jax.random.uniform(lower_key, (NI - PW, PW), jnp.float32, -0.5, 0.5)
    identity = jnp.eye(PW, dtype=jnp.float32)
    symmetric = 0.5 * (upper + upper.T) * (0.4 / PW ** 0.5)
    top_rows = identity * diagonal[:, None] + (1.0 - identity) * symmetric
    return jnp.concatenate([top_rows, lower], axis=0)


def with_ends(array, rng, low, high):
    shape = array.shape
    place = [jax.random.randint(jax.random.fold_in(rng, axis), (), 0, shape[axis]) for axis in range(len(shape))]
    array = array.at[tuple(place)].set(low)
    longest = shape.index(max(shape))
    place[longest] = (place[longest] + 1) % shape[longest]
    return array.at[tuple(place)].set(high)


def setup_inputs(seed: int = 0) -> dict:
    keys = jax.random.split(jax.random.key(seed), 6)
    coupling_blocks = draw_coupling_blocks(jax.random.fold_in(keys[5], 71), 0)
    block_inverse = draw_block_inverse(jax.random.fold_in(keys[5], 71), 0)
    coupling_pattern = with_ends((jax.random.randint(keys[2], (NSUBDOM, CELLS, LINKS + 1), 0, 4) < 3).astype(jnp.int32), jax.random.fold_in(keys[2], 1), 0, 1)
    link_blocks = draw_link_blocks(jax.random.fold_in(keys[5], 71), 0)
    interface_panel = draw_interface_panel(jax.random.fold_in(keys[5], 71), 0)
    return dict(coupling_blocks=coupling_blocks, block_inverse=block_inverse, coupling_pattern=coupling_pattern, link_blocks=link_blocks, interface_panel=interface_panel)


def subdomain_update(blocks, inverse, present):
    masked = blocks * present.astype(jnp.float32)[:, :, None, None]
    solved = jnp.einsum('cjk,cik->cji', inverse, masked[:, 0], precision=lax.Precision.HIGHEST)
    return jnp.einsum('clij,cjk->lik', masked, solved, precision=lax.Precision.HIGHEST)

def reference(coupling_blocks, block_inverse, coupling_pattern, link_blocks, interface_panel):
    updates = lax.map(lambda members: subdomain_update(members[0], members[1], members[2]), (coupling_blocks, block_inverse, coupling_pattern))
    subdomain_count = coupling_blocks.shape[0]
    panel_block = jnp.arange(subdomain_count, dtype=jnp.int32) // SUB_DEV % PBLK
    row_blocks = jnp.concatenate([panel_block[:, None], link_blocks.astype(jnp.int32)], axis=1)
    summed = jnp.zeros((NB_I, PBLK, BLK, BLK), jnp.float32).at[row_blocks, panel_block[:, None]].add(updates)
    summed = summed.transpose(0, 2, 1, 3).reshape(NI, PW)
    schur_panel = interface_panel - summed
    diag_factor = jnp.linalg.cholesky(schur_panel[:PW])
    return lax.linalg.triangular_solve(diag_factor, schur_panel, left_side=False, lower=True, transpose_a=True)
```

```python
import functools

import jax
import jax.numpy as jnp
from jax import lax
from jax.experimental import pallas as pl
from jax.experimental.pallas import tpu as pltpu
from jax.sharding import PartitionSpec as P

F32 = jnp.float32
BF16 = jnp.bfloat16
MESH = pl.DeviceIdType.MESH
BLK = 128
CHUNK = 4
STEP = 16
OFF = ((1, 0), (2, 0), (3, 0), (2, 1), (3, 1), (3, 2))
OFF_AT = {pair: k for k, pair in enumerate(OFF)}


def halves(value):
    high = value.astype(BF16)
    return high, (value - high.astype(F32)).astype(BF16)


def product_nt(a, b):
    ah, al = halves(a)
    bh, bl = halves(b)
    return lax.dot_general(
        jnp.concatenate([ah, al, ah], axis=1),
        jnp.concatenate([bh, bh, bl], axis=1),
        (((1,), (1,)), ((), ())),
        preferred_element_type=F32,
    )


def product_nn(a, b):
    ah, al = halves(a)
    bh, bl = halves(b)
    return jnp.dot(
        jnp.concatenate([ah, al, ah], axis=1),
        jnp.concatenate([bh, bh, bl], axis=0),
        preferred_element_type=F32,
    )


def update_kernel(
    pattern_ref, link_ref, coupling_ref, inverse_ref,
    first_ref, links_ref, slot_ref,
    cbuf, ibuf, lhs, rhs, acc, csem, isem,
):
    subs, cells = coupling_ref.shape[0], coupling_ref.shape[1]
    faces = coupling_ref.shape[2]
    links = faces - 1
    none = subs * links
    rows = faces * BLK

    def fetch(i, carry):
        n, c = i // cells, lax.rem(i, cells)
        pltpu.make_async_copy(inverse_ref.at[n, c], ibuf.at[i], isem.at[i]).start()
        pltpu.make_async_copy(coupling_ref.at[n, c], cbuf.at[i], csem.at[i]).start()
        return carry

    lax.fori_loop(0, subs * cells, fetch, 0)

    def clear(i, carry):
        for n in range(subs):
            slot_ref[n, i] = none
        return carry

    lax.fori_loop(0, slot_ref.shape[1], clear, 0)
    for n in range(subs):
        for l in range(links):
            slot_ref[n, link_ref[n, l]] = n * links + l
    links_ref[none] = jnp.zeros((BLK, BLK), F32)

    for n in range(subs):
        def chunk_step(chunk, carry):
            for k in range(CHUNK):
                cell = chunk * CHUNK + k
                i = n * cells + cell
                pltpu.make_async_copy(inverse_ref.at[n, cell], ibuf.at[i], isem.at[i]).wait()
                pltpu.make_async_copy(coupling_ref.at[n, cell], cbuf.at[i], csem.at[i]).wait()
                for l in range(faces):
                    block = cbuf[i, l] * pattern_ref[n, cell, l].astype(F32)
                    high, low = halves(block)
                    if l == 0:
                        solved = product_nt(ibuf[i], block)
                    place = pl.ds(l * BLK, BLK)
                    lhs[place, pl.ds(k * 2 * BLK, BLK)] = high
                    lhs[place, pl.ds(k * 2 * BLK + BLK, BLK)] = low
                sh, sl = halves(solved)
                rhs[pl.ds(k * 2 * BLK, BLK), :] = jnp.concatenate([sh, sl], axis=1)
                rhs[pl.ds(k * 2 * BLK + BLK, BLK), :] = jnp.concatenate([sh, jnp.zeros_like(sl)], axis=1)
            part = jnp.dot(lhs[...], rhs[...], preferred_element_type=F32)

            @pl.when(chunk == 0)
            def _():
                acc[...] = part

            @pl.when(chunk > 0)
            def _():
                acc[...] += part

            return carry

        lax.fori_loop(0, cells // CHUNK, chunk_step, 0)
        total = acc[:, :BLK] + acc[:, BLK:]
        if n == 0:
            first_ref[...] = total[:BLK]
        else:
            first_ref[...] += total[:BLK]
        links_ref[n * links : (n + 1) * links] = total[BLK:].reshape(links, BLK, BLK)


def local_updates(coupling_blocks, block_inverse, coupling_pattern, link_blocks, block_rows):
    subs, cells, faces = coupling_blocks.shape[:3]
    rows = faces * BLK
    return pl.pallas_call(
        update_kernel,
        out_shape=(
            jax.ShapeDtypeStruct((BLK, BLK), F32),
            jax.ShapeDtypeStruct((subs * (faces - 1) + 1, BLK, BLK), F32),
            jax.ShapeDtypeStruct((subs, block_rows), jnp.int32),
        ),
        in_specs=[
            pl.BlockSpec(memory_space=pltpu.SMEM),
            pl.BlockSpec(memory_space=pltpu.SMEM),
            pl.BlockSpec(memory_space=pl.ANY),
            pl.BlockSpec(memory_space=pl.ANY),
        ],
        out_specs=(
            pl.BlockSpec(memory_space=pltpu.VMEM),
            pl.BlockSpec(memory_space=pltpu.VMEM),
            pl.BlockSpec(memory_space=pltpu.SMEM),
        ),
        scratch_shapes=[
            pltpu.VMEM((subs * cells, faces, BLK, BLK), F32),
            pltpu.VMEM((subs * cells, BLK, BLK), F32),
            pltpu.VMEM((rows, CHUNK * 2 * BLK), BF16),
            pltpu.VMEM((CHUNK * 2 * BLK, 2 * BLK), BF16),
            pltpu.VMEM((rows, 2 * BLK), F32),
            pltpu.SemaphoreType.DMA((subs * cells,)),
            pltpu.SemaphoreType.DMA((subs * cells,)),
        ],
        compiler_params=pltpu.CompilerParams(vmem_limit_bytes=48 << 20),
        name="local_updates",
    )(coupling_pattern, link_blocks, coupling_blocks, block_inverse)


def inverse_factor(pair):
    rows = lax.broadcasted_iota(jnp.int32, (STEP, BLK), 0)
    for r in range(0, BLK, STEP):
        pa, pe = pair[r : r + STEP, :BLK], pair[r : r + STEP, BLK:]
        t = jnp.stack([jnp.broadcast_to(pa[:, r + j : r + j + 1], (STEP, BLK)) for j in range(STEP)])
        for k in range(STEP):
            scale = lax.rsqrt(t[0, k : k + 1, :])
            m = jnp.where(rows > k, t[0] * scale, 0.0)
            if k + 1 < STEP:
                t = t[1:] - m[None] * (t[1:, k : k + 1, :] * scale[None])
            ra, re = pa[k : k + 1] * scale, pe[k : k + 1] * scale
            pa = jnp.where(rows == k, ra, pa - m * ra)
            pe = jnp.where(rows == k, re, pe - m * re)
        pair[r : r + STEP, BLK:] = pe
        if r + STEP < BLK:
            high, low = halves(jnp.concatenate([pa, pe], axis=1))
            ah, al = high[:, :BLK], low[:, :BLK]
            change = lax.dot_general(
                jnp.concatenate([ah, ah, al], axis=0),
                jnp.concatenate([high, low, high], axis=0),
                (((0,), (0,)), ((), ())),
                preferred_element_type=F32,
            )
            pair[r + STEP :, :] = pair[r + STEP :, :] - change[r + STEP :, :]


def panel_kernel(
    nx, slot_ref, first_ref, links_ref, panel_ref, out_ref,
    firstc, gather1, gather2, piece, diag, offpiece, off,
    send0, recv0, acc, relay_r, relay_l, direct_r, direct_l, onward_r, onward_l,
    last, sall, pair, lower, inv, vz, top,
    d1s, d1r, d2s, d2r, d3s, d3r, sc_s, op_r, fw_s, oa_s, oa_r,
    s0s, s0r, s1s, s1r, s2s, s2r, zs, zr,
):
    sub, z = lax.axis_index("sub"), lax.axis_index("blk")
    core = lax.rem(sub, 2)
    x = lax.rem(sub // 2, nx)
    y = sub // (2 * nx)

    def sub_of(yy, xx, cc):
        return (yy * nx + xx) * 2 + cc

    def remote(src, dst, ssem, rsem, to_sub, to_z):
        return pltpu.make_async_remote_copy(
            src_ref=src, dst_ref=dst, send_sem=ssem, recv_sem=rsem,
            device_id=(to_sub, to_z), device_id_type=MESH,
        )

    place = (core * 4 + x) * 4 + z

    def plane_peer(t):
        e = lax.rem(place + t, 32)
        q = e // 4
        return sub_of(y, lax.rem(q, 4), q // 4), lax.rem(e, 4)

    barrier = pltpu.get_barrier_semaphore()

    def greet(t, carry):
        to_sub, to_z = plane_peer(t)
        pl.semaphore_signal(barrier, inc=1, device_id=(to_sub, to_z), device_id_type=MESH)
        return carry

    lax.fori_loop(1, 32, greet, 0)

    def greet_y(t, carry):
        pl.semaphore_signal(
            barrier, inc=1, device_id=(sub_of(lax.rem(y + t, 4), x, core), z), device_id_type=MESH
        )
        return carry

    lax.fori_loop(1, 4, greet_y, 0)

    firstc[...] = -first_ref[...]

    @pl.when(sub == z // 2)
    def _():
        firstc[...] += panel_ref[pl.ds(pl.multiple_of(lax.rem(z, 2) * BLK, BLK), BLK), :]

    pl.semaphore_wait(barrier, 34)

    q = core * 4 + x

    def d1_copy(t):
        to = lax.rem(q + t, 8)
        return remote(
            firstc.at[pl.ds(pl.multiple_of(to * 16, 16), 16)], gather1.at[q],
            d1s.at[t], d1r.at[t], sub_of(y, lax.rem(to, 4), to // 4), z,
        )

    def d2_copy(t):
        return remote(
            gather2.at[y], gather2.at[y], d2s.at[t], d2r.at[t],
            sub_of(lax.rem(y + t, 4), x, core), z,
        )

    mine = pl.ds(pl.multiple_of(q * 16, 16), 16)

    def d3_copy(t):
        to_sub, to_z = plane_peer(t)
        return remote(piece, diag.at[z, mine], d3s.at[t], d3r, to_sub, to_z)

    def loop(low, high, make, *actions):
        def body(t, carry):
            copy = make(t)
            for action in actions:
                getattr(copy, action)()
            return carry

        lax.fori_loop(low, high, body, 0)

    loop(1, 8, d1_copy, "start")
    gather1[q] = firstc[mine, :]

    def scatter(action):
        for k, (i, j) in enumerate(OFF):
            @pl.when((sub == i // 2) & (z == j))
            def _(k=k, i=i, j=j):
                for xx in range(4):
                    src = panel_ref.at[pl.ds((i % 2) * BLK + xx * 32, 32)]
                    if xx == 0 and k % 2 == i // 2 and k // 2 == j:
                        if action == "start":
                            pltpu.make_async_copy(src, offpiece, op_r).start()
                    else:
                        copy = remote(
                            src, offpiece, sc_s.at[k * 4 + xx], op_r,
                            jnp.int32(xx * 2 + k % 2), jnp.int32(k // 2),
                        )
                        getattr(copy, action)()

    scatter("start")

    def placed(r, h, other, to_core):
        to_x = lax.rem(x + r, 4) if h == 0 else other
        to_y = other if h == 0 else lax.rem(y + r, 4)
        g = sub_of(to_y, to_x, to_core) * 2 + h
        return links_ref[slot_ref[0, g]] + links_ref[slot_ref[1, g]]

    def fill(ref, r, to_core):
        def body(other, carry):
            for h in range(2):
                ref[r, h, other] = placed(r, h, other, to_core)
            return carry

        lax.fori_loop(0, 4, body, 0)

    def s0_copy(r):
        return remote(send0.at[r], recv0.at[r], s0s.at[r], s0r.at[r], sub_of(y, x, 1 - core), z)

    for r in (2, 1):
        fill(send0, r, 1 - core)
        s0_copy(r).start()

    loop(1, 8, d1_copy, "wait_recv")
    gather2[y] = jnp.sum(gather1[...], axis=0)
    loop(1, 4, d2_copy, "start")

    for r in (3, 0):
        fill(send0, r, 1 - core)
        s0_copy(r).start()

    holder = z * 2 + core

    def fw_copy(t):
        return remote(offpiece, offpiece, fw_s.at[t], op_r, sub_of(lax.rem(y + t, 4), x, core), z)

    @pl.when(holder < 6)
    def _():
        pltpu.make_async_copy(offpiece, offpiece, op_r).wait()

    @pl.when((holder < 6) & (y == 0))
    def _():
        loop(1, 4, fw_copy, "start")

    loop(1, 4, d2_copy, "wait_recv")
    piece[...] = jnp.sum(gather2[...], axis=0)
    own_diag = pltpu.make_async_copy(piece, diag.at[z, mine], d3r)
    own_diag.start()
    loop(1, 32, d3_copy, "start")

    quarter = pl.ds(pl.multiple_of(x * 32, 32), 32)

    def oa_copy(t):
        to_sub, to_z = plane_peer(t)
        return remote(offpiece, off.at[holder, quarter], oa_s.at[t], oa_r, to_sub, to_z)

    @pl.when(holder < 6)
    def _():
        pltpu.make_async_copy(offpiece, off.at[holder, quarter], oa_r).start()
        loop(1, 32, oa_copy, "start")

    def ring(h, step):
        if h == 0:
            return sub_of(y, lax.rem(x + step + 4, 4), core)
        return sub_of(lax.rem(y + step + 4, 4), x, core)

    def s1_copy(kind, h):
        n = kind * 2 + h
        src, dst, step = (
            (acc.at[2, h, 0:2], relay_r.at[h], 1),
            (acc.at[2, h, 2:4], relay_l.at[h], -1),
            (acc.at[1, h, 2:4], direct_r.at[h], 1),
            (acc.at[3, h, 0:2], direct_l.at[h], -1),
            (acc.at[1, h, 0:2], onward_r.at[h], 1),
            (acc.at[3, h, 2:4], onward_l.at[h], -1),
        )[kind]
        return remote(src, dst, s1s.at[n], s1r.at[n], ring(h, step), z)

    def arrive0(r):
        fill(acc, r, core)
        s0_copy(r).wait_recv()
        acc[r] += recv0[r]

    def service0():
        arrive0(2)
        for h in range(2):
            s1_copy(0, h).start()
            s1_copy(1, h).start()
        arrive0(1)
        for h in range(2):
            s1_copy(2, h).start()
        arrive0(3)
        for h in range(2):
            s1_copy(3, h).start()
        arrive0(0)

    def service1():
        for h in range(2):
            s1_copy(0, h).wait_recv()
            acc[1, h, 0:2] += relay_r[h]
            s1_copy(4, h).start()
            s1_copy(1, h).wait_recv()
            acc[3, h, 2:4] += relay_l[h]
            s1_copy(5, h).start()

    def s2_copy(h, d):
        there = lax.rem((y if h == 0 else x) + d, 4)
        to = sub_of(there, x, core) if h == 0 else sub_of(y, there, core)
        n = h * 3 + d - 1
        return remote(acc.at[0, h, there], last.at[n], s2s.at[n], s2r.at[n], to, z)

    def service2():
        for h in range(2):
            s1_copy(4, h).wait_recv()
            s1_copy(3, h).wait_recv()
            acc[0, h, 0:2] += onward_r[h] + direct_l[h]
            s1_copy(2, h).wait_recv()
            s1_copy(5, h).wait_recv()
            acc[0, h, 2:4] += direct_r[h] + onward_l[h]
            for d in range(1, 4):
                s2_copy(h, d).start()

    def z_copy(d):
        return remote(sall.at[z], sall.at[z], zs.at[d], zr.at[d], sub, z + d)

    def service3():
        for h in range(2):
            total = acc[0, h, y if h == 0 else x]
            for d in range(1, 4):
                s2_copy(h, d).wait_recv()
                total = total + last[h * 3 + d - 1]
            rows = panel_ref[h * BLK : (h + 1) * BLK, :] - total
            sall[z, h * BLK : (h + 1) * BLK] = rows

            @pl.when(sub * 2 + h == z)
            def _():
                sall[z, h * BLK : (h + 1) * BLK] = top[...]

        for d in range(1, 4):
            @pl.when(z + d < 4)
            def _():
                z_copy(d).start()

    service0()

    pltpu.make_async_copy(diag, diag, d3r).wait()
    top[...] = diag[z]
    unit = jnp.where(
        lax.broadcasted_iota(jnp.int32, (BLK, BLK), 0) == lax.broadcasted_iota(jnp.int32, (BLK, BLK), 1),
        1.0, 0.0,
    )
    services = (service1, service2, service3, None)
    for k in range(4):
        pair[:, :BLK] = diag[k]
        pair[:, BLK:] = unit
        inverse_factor(pair)
        w = pair[:, BLK:]
        if k == 0:
            pltpu.make_async_copy(off, off, oa_r).wait()
        for i in range(k + 1, 4):
            lower[OFF_AT[i, k]] = product_nt(off[OFF_AT[i, k]], w)
        for i in range(k + 1, 4):
            for j in range(k + 1, i + 1):
                change = product_nt(lower[OFF_AT[i, k]], lower[OFF_AT[j, k]])
                if i == j:
                    diag[i] = diag[i] - change
                else:
                    off[OFF_AT[i, j]] = off[OFF_AT[i, j]] - change
        for j in range(k):
            part = product_nn(lower[OFF_AT[k, j]], inv[j * 4 + j])
            for m in range(j + 1, k):
                part = part + product_nn(lower[OFF_AT[k, m]], inv[m * 4 + j])
            inv[k * 4 + j] = -product_nn(w, part)
        inv[k * 4 + k] = w

        @pl.when(z == k)
        def _():
            for j in range(k + 1):
                vz[j] = inv[k * 4 + j]

        if services[k] is not None:
            services[k]()

    out_ref[...] = product_nt(sall[z], vz[z])
    for d in range(1, 4):
        @pl.when(z >= d)
        def _():
            remote(sall.at[z - d], sall.at[z - d], zs.at[d], zr.at[d], sub, z).wait_recv()
            out_ref[...] += product_nt(sall[z - d], vz[z - d])

    loop(1, 8, d1_copy, "wait_send")
    loop(1, 4, d2_copy, "wait_send")
    loop(1, 32, d3_copy, "wait_send")
    scatter("wait_send")

    @pl.when((holder < 6) & (y == 0))
    def _():
        loop(1, 4, fw_copy, "wait_send")

    @pl.when(holder < 6)
    def _():
        loop(1, 32, oa_copy, "wait_send")

    for r in range(4):
        s0_copy(r).wait_send()
    for kind in range(6):
        for h in range(2):
            s1_copy(kind, h).wait_send()
    for h in range(2):
        for d in range(1, 4):
            s2_copy(h, d).wait_send()
    for d in range(1, 4):
        @pl.when(z + d < 4)
        def _():
            z_copy(d).wait_send()


def panel_solve(first, links, slots, interface_panel):
    blocks = lambda *lead: pltpu.VMEM((*lead, BLK, BLK), F32)
    dma = lambda n: pltpu.SemaphoreType.DMA((n,))
    return pl.pallas_call(
        functools.partial(panel_kernel, 4),
        out_shape=jax.ShapeDtypeStruct(interface_panel.shape, F32),
        in_specs=[
            pl.BlockSpec(memory_space=pltpu.SMEM),
            pl.BlockSpec(memory_space=pltpu.VMEM),
            pl.BlockSpec(memory_space=pltpu.VMEM),
            pl.BlockSpec(memory_space=pltpu.VMEM),
        ],
        out_specs=pl.BlockSpec(memory_space=pltpu.VMEM),
        scratch_shapes=[
            blocks(),
            pltpu.VMEM((8, 16, BLK), F32),
            pltpu.VMEM((4, 16, BLK), F32),
            pltpu.VMEM((16, BLK), F32),
            blocks(4),
            pltpu.VMEM((32, BLK), F32),
            blocks(6),
            blocks(4, 2, 4), blocks(4, 2, 4), blocks(4, 2, 4),
            blocks(2, 2), blocks(2, 2), blocks(2, 2), blocks(2, 2), blocks(2, 2), blocks(2, 2),
            blocks(6),
            pltpu.VMEM((4, 2 * BLK, BLK), F32),
            pltpu.VMEM((BLK, 2 * BLK), F32),
            blocks(6), blocks(16), blocks(4), blocks(),
            dma(8), dma(8), dma(4), dma(4), dma(32), pltpu.SemaphoreType.DMA,
            dma(24), pltpu.SemaphoreType.DMA, dma(4), dma(32), pltpu.SemaphoreType.DMA,
            dma(4), dma(4), dma(12), dma(12), dma(6), dma(6), dma(4), dma(4),
        ],
        compiler_params=pltpu.CompilerParams(
            collective_id=0, has_side_effects=True, vmem_limit_bytes=48 << 20
        ),
        name="panel_solve",
    )(slots, first, links, interface_panel)


def shards(coupling_blocks, block_inverse, coupling_pattern, link_blocks, interface_panel):
    first, links, slots = local_updates(
        coupling_blocks, block_inverse, coupling_pattern, link_blocks, 64
    )
    return panel_solve(first, links, slots, interface_panel)


def solution(mesh):
    in_specs = (
        P(("sub", "blk"), None, None, None, None),
        P(("sub", "blk"), None, None, None),
        P(("sub", "blk"), None, None),
        P(("sub", "blk"), None),
        P("sub", "blk"),
    )
    out_specs = P("sub", "blk")
    return jax.shard_map(shards, mesh=mesh, in_specs=in_specs, out_specs=out_specs, check_vma=False)
```

```python
import functools

import jax
import jax.numpy as jnp
from jax import lax
from jax.experimental import pallas as pl
from jax.experimental.pallas import tpu as pltpu
from jax.sharding import PartitionSpec as P

F32 = jnp.float32
BF16 = jnp.bfloat16
MESH = pl.DeviceIdType.MESH
BLK = 128
GROUP = 8
STEP = 16
OFF = ((1, 0), (2, 0), (3, 0), (2, 1), (3, 1), (3, 2))
OFF_AT = {pair: k for k, pair in enumerate(OFF)}


def halves(value):
    high = value.astype(BF16)
    return high, (value - high.astype(F32)).astype(BF16)


def product_nt(a, b):
    ah, al = halves(a)
    bh, bl = halves(b)
    return lax.dot_general(
        jnp.concatenate([ah, al, ah], axis=1),
        jnp.concatenate([bh, bh, bl], axis=1),
        (((1,), (1,)), ((), ())),
        preferred_element_type=F32,
    )


def product_nn(a, b):
    ah, al = halves(a)
    bh, bl = halves(b)
    return jnp.dot(
        jnp.concatenate([ah, al, ah], axis=1),
        jnp.concatenate([bh, bh, bl], axis=0),
        preferred_element_type=F32,
    )


def inverse_factor(pair, between):
    rows = lax.broadcasted_iota(jnp.int32, (STEP, BLK), 0)
    for r in range(0, BLK, STEP):
        pa, pe = pair[r : r + STEP, :BLK], pair[r : r + STEP, BLK:]
        t = jnp.stack([jnp.broadcast_to(pa[:, r + j : r + j + 1], (STEP, BLK)) for j in range(STEP)])
        for k in range(STEP):
            scale = lax.rsqrt(t[0, k : k + 1, :])
            m = jnp.where(rows > k, t[0] * scale, 0.0)
            if k + 1 < STEP:
                t = t[1:] - m[None] * (t[1:, k : k + 1, :] * scale[None])
            ra, re = pa[k : k + 1] * scale, pe[k : k + 1] * scale
            pa = jnp.where(rows == k, ra, pa - m * ra)
            pe = jnp.where(rows == k, re, pe - m * re)
        pair[r : r + STEP, BLK:] = pe
        if r + STEP < BLK:
            high, low = halves(jnp.concatenate([pa, pe], axis=1))
            ah, al = high[:, :BLK], low[:, :BLK]
            change = lax.dot_general(
                jnp.concatenate([ah, ah, al], axis=0),
                jnp.concatenate([high, low, high], axis=0),
                (((0,), (0,)), ((), ())),
                preferred_element_type=F32,
            )
            pair[r + STEP :, :] = pair[r + STEP :, :] - change[r + STEP :, :]
        between(r // STEP)


def panel_kernel(
    nx, pattern_ref, link_ref, coupling_ref, inverse_ref, interface_ref, out_ref,
    pattern, link, panel_ref, firsts, faces, inverses, rhs, links_ref, small_s, inv_s, first_s, face_s,
    firstc, gather1, gather2, piece, diag, offpiece, off,
    send0, recv0, acc, relay_r, relay_l, direct_r, direct_l, onward_r, onward_l,
    last, sall, pair, lower, inv, vz, top,
    d1s, d1r, d2s, d2r, d3s, d3r, sc_s, op_r, fw_s, oa_s, oa_r,
    s0s, s0r, s1s, s1r, s2s, s2r, zs, zr,
):
    sub, z = lax.axis_index("sub"), lax.axis_index("blk")
    core = lax.rem(sub, 2)
    x = lax.rem(sub // 2, nx)
    y = sub // (2 * nx)

    def sub_of(yy, xx, cc):
        return (yy * nx + xx) * 2 + cc

    def remote(src, dst, ssem, rsem, to_sub, to_z):
        return pltpu.make_async_remote_copy(
            src_ref=src, dst_ref=dst, send_sem=ssem, recv_sem=rsem,
            device_id=(to_sub, to_z), device_id_type=MESH,
        )

    place = (core * 4 + x) * 4 + z

    def plane_peer(t):
        e = lax.rem(place + t, 32)
        q = e // 4
        return sub_of(y, lax.rem(q, 4), q // 4), lax.rem(e, 4)

    barrier = pltpu.get_barrier_semaphore()

    def greet(t, carry):
        to_sub, to_z = plane_peer(t)
        pl.semaphore_signal(barrier, inc=1, device_id=(to_sub, to_z), device_id_type=MESH)
        return carry

    lax.fori_loop(1, 32, greet, 0)

    def greet_y(t, carry):
        pl.semaphore_signal(
            barrier, inc=1, device_id=(sub_of(lax.rem(y + t, 4), x, core), z), device_id_type=MESH
        )
        return carry

    lax.fori_loop(1, 4, greet_y, 0)

    subs, cells, links = coupling_ref.shape[0], coupling_ref.shape[1], coupling_ref.shape[2] - 1
    per_sub = cells // GROUP
    none = subs * links
    small = [
        pltpu.make_async_copy(pattern_ref, pattern, small_s.at[0]),
        pltpu.make_async_copy(link_ref, link, small_s.at[1]),
        pltpu.make_async_copy(interface_ref, panel_ref, small_s.at[2]),
    ]
    inv_in, first_in, face_in = [], [], []
    for g in range(subs * per_sub):
        n, c = g // per_sub, pl.ds(g % per_sub * GROUP, GROUP)
        held = pl.ds(g * GROUP, GROUP)
        inv_in.append(pltpu.make_async_copy(inverse_ref.at[n, c], inverses.at[held], inv_s.at[g]))
        first_in.append(pltpu.make_async_copy(coupling_ref.at[n, c, 0], firsts.at[held], first_s.at[g]))
        face_in.append(
            pltpu.make_async_copy(coupling_ref.at[n, c, pl.ds(1, links)], faces.at[held], face_s.at[g])
        )
    for copy in small + [copy for both in zip(inv_in, first_in) for copy in both] + face_in:
        copy.start()
    links_ref[none] = jnp.zeros((BLK, BLK), F32)

    zero = jnp.zeros((BLK, BLK), BF16)
    small[0].wait()
    for g in range(subs * per_sub):
        inv_in[g].wait()
        first_in[g].wait()
        left, right = [], []
        for i in range(g * GROUP, g * GROUP + GROUP):
            bh, bl = halves(firsts[i] * pattern[0, i // cells, i % cells].astype(F32))
            ih, il = halves(inverses[i])
            weight = jnp.concatenate(
                [jnp.concatenate([bh, bh], axis=1), jnp.concatenate([bl, zero], axis=1)], axis=0
            )
            both = lax.dot_general(
                jnp.concatenate([ih, il], axis=1), weight, (((1,), (1,)), ((), ())),
                preferred_element_type=F32,
            )
            sh, sl = halves(both[:, :BLK] + both[:, BLK:])
            pair_hl = jnp.concatenate([sh, sl], axis=1)
            rhs[i] = pair_hl
            left += [bh, bl]
            right += [pair_hl, jnp.concatenate([sh, zero], axis=1)]
        both = jnp.dot(
            jnp.concatenate(left, axis=1), jnp.concatenate(right, axis=0), preferred_element_type=F32
        )
        part = both[:, :BLK] + both[:, BLK:]
        firstc[...] = -part if g == 0 else firstc[...] - part

    def link_updates(g):
        face_in[g].wait()
        n = g // per_sub
        highs, lows = [], []
        for i in range(g * GROUP, g * GROUP + GROUP):
            value = jnp.concatenate(
                [faces[i, l] * pattern[l + 1, n, i % cells].astype(F32) for l in range(links)], axis=0
            )
            high, low = halves(value)
            highs.append(high)
            lows.append(low)
        right = rhs[g * GROUP : (g + 1) * GROUP].reshape(GROUP * BLK, 2 * BLK)
        both = jnp.dot(jnp.concatenate(highs, axis=1), right, preferred_element_type=F32)
        rest = jnp.dot(jnp.concatenate(lows, axis=1), right[:, :BLK], preferred_element_type=F32)
        part = (both[:, :BLK] + both[:, BLK:] + rest).reshape(links, BLK, BLK)
        held = pl.ds(n * links, links)
        links_ref[held] = part if g % per_sub == 0 else links_ref[held] + part

    small[1].wait()
    small[2].wait()

    @pl.when(sub == z // 2)
    def _():
        firstc[...] += panel_ref[pl.ds(pl.multiple_of(lax.rem(z, 2) * BLK, BLK), BLK), :]

    pl.semaphore_wait(barrier, 34)

    q = core * 4 + x

    def d1_copy(t):
        to = lax.rem(q + t, 8)
        return remote(
            firstc.at[pl.ds(pl.multiple_of(to * 16, 16), 16)], gather1.at[q],
            d1s.at[t], d1r.at[t], sub_of(y, lax.rem(to, 4), to // 4), z,
        )

    def d2_copy(t):
        return remote(
            gather2.at[y], gather2.at[y], d2s.at[t], d2r.at[t],
            sub_of(lax.rem(y + t, 4), x, core), z,
        )

    mine = pl.ds(pl.multiple_of(q * 16, 16), 16)

    def d3_copy(t):
        to_sub, to_z = plane_peer(t)
        return remote(piece, diag.at[z, mine], d3s.at[t], d3r, to_sub, to_z)

    def loop(low, high, make, *actions):
        def body(t, carry):
            copy = make(t)
            for action in actions:
                getattr(copy, action)()
            return carry

        lax.fori_loop(low, high, body, 0)

    loop(1, 8, d1_copy, "start")
    gather1[q] = firstc[mine, :]

    def scatter(action):
        for k, (i, j) in enumerate(OFF):
            @pl.when((sub == i // 2) & (z == j))
            def _(k=k, i=i, j=j):
                for xx in range(4):
                    src = panel_ref.at[pl.ds((i % 2) * BLK + xx * 32, 32)]
                    if xx == 0 and k % 2 == i // 2 and k // 2 == j:
                        if action == "start":
                            pltpu.make_async_copy(src, offpiece, op_r).start()
                    else:
                        copy = remote(
                            src, offpiece, sc_s.at[k * 4 + xx], op_r,
                            jnp.int32(xx * 2 + k % 2), jnp.int32(k // 2),
                        )
                        getattr(copy, action)()

    scatter("start")

    link_updates(0)
    loop(1, 8, d1_copy, "wait_recv")
    gather2[y] = jnp.sum(gather1[...], axis=0)
    loop(1, 4, d2_copy, "start")

    link_updates(1)

    holder = z * 2 + core

    def fw_copy(t):
        return remote(offpiece, offpiece, fw_s.at[t], op_r, sub_of(lax.rem(y + t, 4), x, core), z)

    @pl.when(holder < 6)
    def _():
        pltpu.make_async_copy(offpiece, offpiece, op_r).wait()

    @pl.when((holder < 6) & (y == 0))
    def _():
        loop(1, 4, fw_copy, "start")

    loop(1, 4, d2_copy, "wait_recv")
    piece[...] = jnp.sum(gather2[...], axis=0)
    own_diag = pltpu.make_async_copy(piece, diag.at[z, mine], d3r)
    own_diag.start()
    loop(1, 32, d3_copy, "start")

    link_updates(2)

    quarter = pl.ds(pl.multiple_of(x * 32, 32), 32)

    def oa_copy(t):
        to_sub, to_z = plane_peer(t)
        return remote(offpiece, off.at[holder, quarter], oa_s.at[t], oa_r, to_sub, to_z)

    @pl.when(holder < 6)
    def _():
        pltpu.make_async_copy(offpiece, off.at[holder, quarter], oa_r).start()
        loop(1, 32, oa_copy, "start")

    link_updates(3)

    names = [[link[n, l] for l in range(links)] for n in range(subs)]

    def slot(n, g):
        found = jnp.int32(none)
        for l in range(links):
            found = jnp.where(names[n][l] == g, n * links + l, found)
        return found

    def placed(r, h, other, to_core):
        to_x = lax.rem(x + r, 4) if h == 0 else other
        to_y = other if h == 0 else lax.rem(y + r, 4)
        g = sub_of(to_y, to_x, to_core) * 2 + h
        return links_ref[slot(0, g)] + links_ref[slot(1, g)]

    def fill(ref, r, to_core):
        def body(other, carry):
            for h in range(2):
                ref[r, h, other] = placed(r, h, other, to_core)
            return carry

        lax.fori_loop(0, 4, body, 0)

    def s0_copy(r):
        return remote(send0.at[r], recv0.at[r], s0s.at[r], s0r.at[r], sub_of(y, x, 1 - core), z)

    for r in (2, 1, 3, 0):
        fill(send0, r, 1 - core)
        s0_copy(r).start()

    def ring(h, step):
        if h == 0:
            return sub_of(y, lax.rem(x + step + 4, 4), core)
        return sub_of(lax.rem(y + step + 4, 4), x, core)

    def s1_copy(kind, h):
        n = kind * 2 + h
        src, dst, step = (
            (acc.at[2, h, 0:2], relay_r.at[h], 1),
            (acc.at[2, h, 2:4], relay_l.at[h], -1),
            (acc.at[1, h, 2:4], direct_r.at[h], 1),
            (acc.at[3, h, 0:2], direct_l.at[h], -1),
            (acc.at[1, h, 0:2], onward_r.at[h], 1),
            (acc.at[3, h, 2:4], onward_l.at[h], -1),
        )[kind]
        return remote(src, dst, s1s.at[n], s1r.at[n], ring(h, step), z)

    def arrive0(r):
        fill(acc, r, core)
        s0_copy(r).wait_recv()
        acc[r] += recv0[r]

    def service0(r):
        arrive0(r)
        if r:
            for kind in {2: (0, 1), 1: (2,), 3: (3,)}[r]:
                for h in range(2):
                    s1_copy(kind, h).start()

    def service1():
        for h in range(2):
            s1_copy(0, h).wait_recv()
            acc[1, h, 0:2] += relay_r[h]
            s1_copy(4, h).start()
            s1_copy(1, h).wait_recv()
            acc[3, h, 2:4] += relay_l[h]
            s1_copy(5, h).start()

    def s2_copy(h, d):
        there = lax.rem((y if h == 0 else x) + d, 4)
        to = sub_of(there, x, core) if h == 0 else sub_of(y, there, core)
        n = h * 3 + d - 1
        return remote(acc.at[0, h, there], last.at[n], s2s.at[n], s2r.at[n], to, z)

    def service2():
        for h in range(2):
            s1_copy(4, h).wait_recv()
            s1_copy(3, h).wait_recv()
            acc[0, h, 0:2] += onward_r[h] + direct_l[h]
            s1_copy(2, h).wait_recv()
            s1_copy(5, h).wait_recv()
            acc[0, h, 2:4] += direct_r[h] + onward_l[h]
            for d in range(1, 4):
                s2_copy(h, d).start()

    def z_copy(d):
        return remote(sall.at[z], sall.at[z], zs.at[d], zr.at[d], sub, z + d)

    def service3():
        for h in range(2):
            total = acc[0, h, y if h == 0 else x]
            for d in range(1, 4):
                s2_copy(h, d).wait_recv()
                total = total + last[h * 3 + d - 1]
            rows = panel_ref[h * BLK : (h + 1) * BLK, :] - total
            sall[z, h * BLK : (h + 1) * BLK] = rows

            @pl.when(sub * 2 + h == z)
            def _():
                sall[z, h * BLK : (h + 1) * BLK] = top[...]

        for d in range(1, 4):
            @pl.when(z + d < 4)
            def _():
                z_copy(d).start()

    pltpu.make_async_copy(diag, diag, d3r).wait()
    top[...] = diag[z]
    unit = jnp.where(
        lax.broadcasted_iota(jnp.int32, (BLK, BLK), 0) == lax.broadcasted_iota(jnp.int32, (BLK, BLK), 1),
        1.0, 0.0,
    )
    hooks = {
        (0, 1): lambda: service0(2),
        (0, 3): lambda: service0(1),
        (0, 5): lambda: service0(3),
        (0, 7): lambda: service0(0),
        (1, 3): service1,
        (2, 5): service2,
        (3, 2): service3,
    }
    for k in range(4):
        pair[:, :BLK] = diag[k]
        pair[:, BLK:] = unit
        inverse_factor(pair, lambda r, k=k: hooks.get((k, r), lambda: None)())
        w = pair[:, BLK:]
        if k == 0:
            pltpu.make_async_copy(off, off, oa_r).wait()
        for i in range(k + 1, 4):
            lower[OFF_AT[i, k]] = product_nt(off[OFF_AT[i, k]], w)
        for i in range(k + 1, 4):
            for j in range(k + 1, i + 1):
                change = product_nt(lower[OFF_AT[i, k]], lower[OFF_AT[j, k]])
                if i == j:
                    diag[i] = diag[i] - change
                else:
                    off[OFF_AT[i, j]] = off[OFF_AT[i, j]] - change
        for j in range(k):
            part = product_nn(lower[OFF_AT[k, j]], inv[j * 4 + j])
            for m in range(j + 1, k):
                part = part + product_nn(lower[OFF_AT[k, m]], inv[m * 4 + j])
            inv[k * 4 + j] = -product_nn(w, part)
        inv[k * 4 + k] = w

        @pl.when(z == k)
        def _():
            for j in range(k + 1):
                vz[j] = inv[k * 4 + j]

    out_ref[...] = product_nt(sall[z], vz[z])
    for d in range(1, 4):
        @pl.when(z >= d)
        def _():
            remote(sall.at[z - d], sall.at[z - d], zs.at[d], zr.at[d], sub, z).wait_recv()
            out_ref[...] += product_nt(sall[z - d], vz[z - d])

    loop(1, 8, d1_copy, "wait_send")
    loop(1, 4, d2_copy, "wait_send")
    loop(1, 32, d3_copy, "wait_send")
    scatter("wait_send")

    @pl.when((holder < 6) & (y == 0))
    def _():
        loop(1, 4, fw_copy, "wait_send")

    @pl.when(holder < 6)
    def _():
        loop(1, 32, oa_copy, "wait_send")

    for r in range(4):
        s0_copy(r).wait_send()
    for kind in range(6):
        for h in range(2):
            s1_copy(kind, h).wait_send()
    for h in range(2):
        for d in range(1, 4):
            s2_copy(h, d).wait_send()
    for d in range(1, 4):
        @pl.when(z + d < 4)
        def _():
            z_copy(d).wait_send()


def panel_solve(pattern, link, coupling, inverse, interface):
    subs, cells, faces = coupling.shape[:3]
    blocks = lambda *lead: pltpu.VMEM((*lead, BLK, BLK), F32)
    dma = lambda n: pltpu.SemaphoreType.DMA((n,))
    groups = subs * cells // GROUP
    return pl.pallas_call(
        functools.partial(panel_kernel, 4),
        out_shape=jax.ShapeDtypeStruct(interface.shape, F32),
        in_specs=[pl.BlockSpec(memory_space=pltpu.HBM)] * 5,
        out_specs=pl.BlockSpec(memory_space=pltpu.VMEM),
        scratch_shapes=[
            pltpu.SMEM(pattern.shape, jnp.int32),
            pltpu.SMEM(link.shape, jnp.int32),
            pltpu.VMEM(interface.shape, F32),
            blocks(subs * cells),
            blocks(subs * cells, faces - 1),
            blocks(subs * cells),
            pltpu.VMEM((subs * cells, BLK, 2 * BLK), BF16),
            blocks(subs * (faces - 1) + 1),
            dma(3), dma(groups), dma(groups), dma(groups),
            blocks(),
            pltpu.VMEM((8, 16, BLK), F32),
            pltpu.VMEM((4, 16, BLK), F32),
            pltpu.VMEM((16, BLK), F32),
            blocks(4),
            pltpu.VMEM((32, BLK), F32),
            blocks(6),
            blocks(4, 2, 4), blocks(4, 2, 4), blocks(4, 2, 4),
            blocks(2, 2), blocks(2, 2), blocks(2, 2), blocks(2, 2), blocks(2, 2), blocks(2, 2),
            blocks(6),
            pltpu.VMEM((4, 2 * BLK, BLK), F32),
            pltpu.VMEM((BLK, 2 * BLK), F32),
            blocks(6), blocks(16), blocks(4), blocks(),
            dma(8), dma(8), dma(4), dma(4), dma(32), pltpu.SemaphoreType.DMA,
            dma(24), pltpu.SemaphoreType.DMA, dma(4), dma(32), pltpu.SemaphoreType.DMA,
            dma(4), dma(4), dma(12), dma(12), dma(6), dma(6), dma(4), dma(4),
        ],
        compiler_params=pltpu.CompilerParams(
            collective_id=0, has_side_effects=True, vmem_limit_bytes=60 << 20
        ),
        name="panel_solve",
    )(pattern, link, coupling, inverse, interface)


def shards(coupling_blocks, block_inverse, coupling_pattern, link_blocks, interface_panel):
    pattern = coupling_pattern.transpose(2, 0, 1)
    return panel_solve(pattern, link_blocks, coupling_blocks, block_inverse, interface_panel)


def solution(mesh):
    in_specs = (
        P(("sub", "blk"), None, None, None, None),
        P(("sub", "blk"), None, None, None),
        P(("sub", "blk"), None, None),
        P(("sub", "blk"), None),
        P("sub", "blk"),
    )
    out_specs = P("sub", "blk")
    return jax.shard_map(shards, mesh=mesh, in_specs=in_specs, out_specs=out_specs, check_vma=False)
```

```python
import functools

import jax
import jax.numpy as jnp
from jax import lax
from jax.experimental import pallas as pl
from jax.experimental.pallas import tpu as pltpu
from jax.sharding import PartitionSpec as P

F32 = jnp.float32
BF16 = jnp.bfloat16
MESH = pl.DeviceIdType.MESH
BLK = 128
GROUP = 8
STEP = 16
OFF = ((1, 0), (2, 0), (3, 0), (2, 1), (3, 1), (3, 2))
OFF_AT = {pair: k for k, pair in enumerate(OFF)}


def halves(value):
    high = value.astype(BF16)
    return high, (value - high.astype(F32)).astype(BF16)


def product_nt(a, b):
    ah, al = halves(a)
    bh, bl = halves(b)
    return lax.dot_general(
        jnp.concatenate([ah, al, ah], axis=1),
        jnp.concatenate([bh, bh, bl], axis=1),
        (((1,), (1,)), ((), ())),
        preferred_element_type=F32,
    )


def product_nn(a, b):
    ah, al = halves(a)
    bh, bl = halves(b)
    return jnp.dot(
        jnp.concatenate([ah, al, ah], axis=1),
        jnp.concatenate([bh, bh, bl], axis=0),
        preferred_element_type=F32,
    )


def inverse_factor(pair, between):
    rows = lax.broadcasted_iota(jnp.int32, (STEP, BLK), 0)
    for r in range(0, BLK, STEP):
        pa, pe = pair[r : r + STEP, :BLK], pair[r : r + STEP, BLK:]
        t = jnp.stack([jnp.broadcast_to(pa[:, r + j : r + j + 1], (STEP, BLK)) for j in range(STEP)])
        for k in range(STEP):
            scale = lax.rsqrt(t[0, k : k + 1, :])
            m = jnp.where(rows > k, t[0] * scale, 0.0)
            if k + 1 < STEP:
                t = t[1:] - m[None] * (t[1:, k : k + 1, :] * scale[None])
            ra, re = pa[k : k + 1] * scale, pe[k : k + 1] * scale
            pa = jnp.where(rows == k, ra, pa - m * ra)
            pe = jnp.where(rows == k, re, pe - m * re)
        pair[r : r + STEP, BLK:] = pe
        if r + STEP < BLK:
            high, low = halves(jnp.concatenate([pa, pe], axis=1))
            ah, al = high[:, :BLK], low[:, :BLK]
            change = lax.dot_general(
                jnp.concatenate([ah, ah, al], axis=0),
                jnp.concatenate([high, low, high], axis=0),
                (((0,), (0,)), ((), ())),
                preferred_element_type=F32,
            )
            pair[r + STEP :, :] = pair[r + STEP :, :] - change[r + STEP :, :]
        between(r // STEP)


def panel_kernel(
    nx, pattern_ref, link_ref, coupling_ref, inverse_ref, interface_ref, out_ref,
    pattern, link, peer_link, panel_ref, firsts, faces, inverses, rhs, links_ref, peer_links,
    small_s, inv_s, first_s, face_s,
    firstc, gather1, gather2, pieces, top_cols,
    acc, relay_r, relay_l, direct_r, direct_l, onward_r, onward_l,
    last, sall, pair, lower, inv, vz, top,
    d1s, d1r, d2s, d2r, d3s, d3r, sc_s, op_r, fw_s,
    s0s, s0r, s1s, s1r, s2s, s2r, zs, zr,
):
    sub, z = lax.axis_index("sub"), lax.axis_index("blk")
    core = lax.rem(sub, 2)
    x = lax.rem(sub // 2, nx)
    y = sub // (2 * nx)

    def sub_of(yy, xx, cc):
        return (yy * nx + xx) * 2 + cc

    def remote(src, dst, ssem, rsem, to_sub, to_z):
        return pltpu.make_async_remote_copy(
            src_ref=src, dst_ref=dst, send_sem=ssem, recv_sem=rsem,
            device_id=(to_sub, to_z), device_id_type=MESH,
        )

    q = core * 4 + x

    def row_peer(t):
        to = lax.rem(q + t, 8)
        return to, sub_of(y, lax.rem(to, 4), to // 4)

    def y_peer(t):
        return sub_of(lax.rem(y + t, 4), x, core)

    barrier = pltpu.get_barrier_semaphore()

    def greet(to_sub, to_z):
        pl.semaphore_signal(barrier, inc=1, device_id=(to_sub, to_z), device_id_type=MESH)

    for t in range(1, 8):
        greet(row_peer(t)[1], z)
    for t in range(1, 4):
        greet(y_peer(t), z)
        greet(sub, lax.rem(z + t, 4))

    subs, cells, links = coupling_ref.shape[0], coupling_ref.shape[1], coupling_ref.shape[2] - 1
    per_sub = cells // GROUP
    none = subs * links
    small = [
        pltpu.make_async_copy(pattern_ref, pattern, small_s.at[0]),
        pltpu.make_async_copy(link_ref, link, small_s.at[1]),
        pltpu.make_async_copy(interface_ref, panel_ref, small_s.at[2]),
    ]
    inv_in, first_in, face_in = [], [], []
    for g in range(subs * per_sub):
        n, c = g // per_sub, pl.ds(g % per_sub * GROUP, GROUP)
        held = pl.ds(g * GROUP, GROUP)
        inv_in.append(pltpu.make_async_copy(inverse_ref.at[n, c], inverses.at[held], inv_s.at[g]))
        first_in.append(pltpu.make_async_copy(coupling_ref.at[n, c, 0], firsts.at[held], first_s.at[g]))
        face_in.append(
            pltpu.make_async_copy(coupling_ref.at[n, c, pl.ds(1, links)], faces.at[held], face_s.at[g])
        )
    for copy in small + [copy for both in zip(inv_in, first_in) for copy in both] + face_in:
        copy.start()
    links_ref[none] = jnp.zeros((BLK, BLK), F32)
    peer_links[none] = jnp.zeros((BLK, BLK), F32)

    zero = jnp.zeros((BLK, BLK), BF16)
    small[0].wait()
    for g in range(subs * per_sub):
        inv_in[g].wait()
        first_in[g].wait()
        left, right = [], []
        for i in range(g * GROUP, g * GROUP + GROUP):
            bh, bl = halves(firsts[i] * pattern[0, i // cells, i % cells].astype(F32))
            ih, il = halves(inverses[i])
            weight = jnp.concatenate(
                [jnp.concatenate([bh, bh], axis=1), jnp.concatenate([bl, zero], axis=1)], axis=0
            )
            both = lax.dot_general(
                jnp.concatenate([ih, il], axis=1), weight, (((1,), (1,)), ((), ())),
                preferred_element_type=F32,
            )
            sh, sl = halves(both[:, :BLK] + both[:, BLK:])
            pair_hl = jnp.concatenate([sh, sl], axis=1)
            rhs[i] = pair_hl
            left += [bh, bl]
            right += [pair_hl, jnp.concatenate([sh, zero], axis=1)]
        both = jnp.dot(
            jnp.concatenate(left, axis=1), jnp.concatenate(right, axis=0), preferred_element_type=F32
        )
        part = both[:, :BLK] + both[:, BLK:]
        firstc[...] = -part if g == 0 else firstc[...] - part

    def link_updates(g):
        face_in[g].wait()
        n = g // per_sub
        highs, lows = [], []
        for i in range(g * GROUP, g * GROUP + GROUP):
            value = jnp.concatenate(
                [faces[i, l] * pattern[l + 1, n, i % cells].astype(F32) for l in range(links)], axis=0
            )
            high, low = halves(value)
            highs.append(high)
            lows.append(low)
        right = rhs[g * GROUP : (g + 1) * GROUP].reshape(GROUP * BLK, 2 * BLK)
        both = jnp.dot(jnp.concatenate(highs, axis=1), right, preferred_element_type=F32)
        rest = jnp.dot(jnp.concatenate(lows, axis=1), right[:, :BLK], preferred_element_type=F32)
        part = (both[:, :BLK] + both[:, BLK:] + rest).reshape(links, BLK, BLK)
        held = pl.ds(n * links, links)
        links_ref[held] = part if g % per_sub == 0 else links_ref[held] + part

    small[1].wait()
    small[2].wait()

    @pl.when(sub == z // 2)
    def _():
        firstc[...] += panel_ref[lax.rem(z, 2)]

    pl.semaphore_wait(barrier, 13)

    mine = pl.ds(pl.multiple_of(q * 16, 16), 16)

    def landed(ref, sem):
        pltpu.make_async_copy(ref, ref, sem).wait()

    for t in range(1, 8):
        to, to_sub = row_peer(t)
        remote(
            firstc.at[pl.ds(pl.multiple_of(to * 16, 16), 16)], gather1.at[q], d1s, d1r, to_sub, z
        ).start()
    gather1[q] = firstc[mine, :]

    SOURCES = ((0, 0, 1, 2), (1, 0, 0, 2), (1, 1, 0, 2), (1, 2, 1, 2))

    def source_copy(t, owner, low, high):
        to, to_sub = row_peer(t)
        src = panel_ref.at[low:high, pl.ds(pl.multiple_of(to * 16, 16), 16)]
        dst = pieces.at[2 * owner + low : 2 * owner + high]
        if t == 0:
            return pltpu.make_async_copy(src, dst, op_r)
        return remote(src, dst, sc_s, op_r, to_sub, z)

    for owner, column, low, high in SOURCES:
        @pl.when((sub == owner) & (z == column))
        def _(owner=owner, low=low, high=high):
            for t in range(8):
                source_copy(t, owner, low, high).start()

    peer = sub_of(y, x, 1 - core)
    link_copy = remote(link, peer_link, s0s.at[2], s0r.at[2], peer, z)
    link_copy.start()

    def s0_copy(n):
        part = pl.ds(n * links, links)
        return remote(links_ref.at[part], peer_links.at[part], s0s.at[n], s0r.at[n], peer, z)

    def fw_copy(t, column):
        part = pieces.at[column + 1 : 4]
        return remote(part, part, fw_s.at[t], op_r, y_peer(t), z)

    link_updates(0)
    link_updates(1)
    s0_copy(0).start()

    landed(gather1.at[0:7], d1r)
    gather2[y] = jnp.sum(gather1[...], axis=0)
    for t in range(1, 4):
        remote(gather2.at[y], gather2.at[y], d2s, d2r, y_peer(t), z).start()
    for column in range(3):
        @pl.when((z == column) & (y == 0))
        def _(column=column):
            landed(pieces.at[column + 1 : 4], op_r)
            for t in range(1, 4):
                fw_copy(t, column).start()

    link_updates(2)
    link_updates(3)
    s0_copy(1).start()

    landed(gather2.at[0:3], d2r)
    pieces[z] = jnp.sum(gather2[...], axis=0)
    for column in range(3):
        @pl.when((z == column) & (y > 0))
        def _(column=column):
            landed(pieces.at[column + 1 : 4], op_r)

    pltpu.make_async_copy(pieces.at[z], top_cols.at[z, z, mine], d3r.at[z]).start()
    for ahead in range(3, -1, -1):
        @pl.when(z + ahead < 4)
        def _(ahead=ahead):
            part = pl.ds(z, ahead + 1)

            def send(t, carry):
                remote(
                    pieces.at[part], top_cols.at[z, part, mine], d3s.at[ahead], d3r.at[z],
                    row_peer(t)[1], z + ahead,
                ).start()
                return carry

            lax.fori_loop(0 if ahead else 1, 8, send, 0)

    def column_arrives(j):
        for row in range(j, 4):
            @pl.when(z == row)
            def _(row=row):
                landed(top_cols.at[j, j : row + 1], d3r.at[j])

    link_copy.wait_recv()
    names = [[link[n, l] for l in range(links)] for n in range(subs)]
    peer_names = [[peer_link[n, l] for l in range(links)] for n in range(subs)]

    def slot(names, n, g):
        found = jnp.int32(none)
        for l in range(links):
            found = jnp.where(names[n][l] == g, n * links + l, found)
        return found

    def fill(r):
        def body(other, carry):
            for h in range(2):
                to_x = lax.rem(x + r, 4) if h == 0 else other
                to_y = other if h == 0 else lax.rem(y + r, 4)
                g = sub_of(to_y, to_x, core) * 2 + h
                total = links_ref[slot(names, 0, g)]
                for n in range(1, subs):
                    total = total + links_ref[slot(names, n, g)]
                for n in range(subs):
                    total = total + peer_links[slot(peer_names, n, g)]
                acc[r, h, other] = total
            return carry

        lax.fori_loop(0, 4, body, 0)

    def ring(h, step):
        if h == 0:
            return sub_of(y, lax.rem(x + step + 4, 4), core)
        return sub_of(lax.rem(y + step + 4, 4), x, core)

    def s1_copy(kind, h):
        n = kind * 2 + h
        src, dst, step = (
            (acc.at[2, h, 0:2], relay_r.at[h], 1),
            (acc.at[2, h, 2:4], relay_l.at[h], -1),
            (acc.at[1, h, 2:4], direct_r.at[h], 1),
            (acc.at[3, h, 0:2], direct_l.at[h], -1),
            (acc.at[1, h, 0:2], onward_r.at[h], 1),
            (acc.at[3, h, 2:4], onward_l.at[h], -1),
        )[kind]
        return remote(src, dst, s1s.at[n], s1r.at[n], ring(h, step), z)

    for n in range(subs):
        s0_copy(n).wait_recv()
    for r, kinds in ((2, (0, 1)), (1, (2,)), (3, (3,)), (0, ())):
        fill(r)
        for kind in kinds:
            for h in range(2):
                s1_copy(kind, h).start()

    def service1():
        for h in range(2):
            s1_copy(0, h).wait_recv()
            acc[1, h, 0:2] += relay_r[h]
            s1_copy(4, h).start()
            s1_copy(1, h).wait_recv()
            acc[3, h, 2:4] += relay_l[h]
            s1_copy(5, h).start()

    def s2_copy(h, d):
        there = lax.rem((y if h == 0 else x) + d, 4)
        to = sub_of(there, x, core) if h == 0 else sub_of(y, there, core)
        n = h * 3 + d - 1
        return remote(acc.at[0, h, there], last.at[n], s2s.at[n], s2r.at[n], to, z)

    def service2():
        for h in range(2):
            s1_copy(4, h).wait_recv()
            s1_copy(3, h).wait_recv()
            acc[0, h, 0:2] += onward_r[h] + direct_l[h]
            s1_copy(2, h).wait_recv()
            s1_copy(5, h).wait_recv()
            acc[0, h, 2:4] += direct_r[h] + onward_l[h]
            for d in range(1, 4):
                s2_copy(h, d).start()

    def z_copy(d):
        return remote(sall.at[z], sall.at[z], zs.at[d], zr.at[d], sub, z + d)

    def service3():
        for h in range(2):
            total = acc[0, h, y if h == 0 else x]
            for d in range(1, 4):
                s2_copy(h, d).wait_recv()
                total = total + last[h * 3 + d - 1]
            rows = panel_ref[h] - total
            sall[z, h * BLK : (h + 1) * BLK] = rows

            @pl.when(sub * 2 + h == z)
            def _():
                sall[z, h * BLK : (h + 1) * BLK] = top[...]

        for d in range(1, 4):
            @pl.when(z + d < 4)
            def _():
                z_copy(d).start()

    column_arrives(0)
    unit = jnp.where(
        lax.broadcasted_iota(jnp.int32, (BLK, BLK), 0) == lax.broadcasted_iota(jnp.int32, (BLK, BLK), 1),
        1.0, 0.0,
    )
    hooks = {
        (0, 3): service1,
        (1, 3): service2,
        (2, 4): service3,
    }
    for k in range(4):
        pair[:, :BLK] = top_cols[k, k]
        pair[:, BLK:] = unit
        inverse_factor(pair, lambda r, k=k: hooks.get((k, r), lambda: None)())
        w = pair[:, BLK:]
        if k == 0:
            for j in range(1, 4):
                column_arrives(j)
            top[...] = top_cols[z, z]
        for i in range(k + 1, 4):
            lower[OFF_AT[i, k]] = product_nt(top_cols[k, i], w)
        for i in range(k + 1, 4):
            for j in range(k + 1, i + 1):
                change = product_nt(lower[OFF_AT[i, k]], lower[OFF_AT[j, k]])
                top_cols[j, i] = top_cols[j, i] - change
        for j in range(k):
            part = product_nn(lower[OFF_AT[k, j]], inv[j * 4 + j])
            for m in range(j + 1, k):
                part = part + product_nn(lower[OFF_AT[k, m]], inv[m * 4 + j])
            inv[k * 4 + j] = -product_nn(w, part)
        inv[k * 4 + k] = w

        @pl.when(z == k)
        def _():
            for j in range(k + 1):
                vz[j] = inv[k * 4 + j]

    out_ref[...] = product_nt(sall[z], vz[z])
    for d in range(1, 4):
        @pl.when(z >= d)
        def _():
            remote(sall.at[z - d], sall.at[z - d], zs.at[d], zr.at[d], sub, z).wait_recv()
            out_ref[...] += product_nt(sall[z - d], vz[z - d])

    landed(gather1.at[0:7], d1s)
    landed(gather2.at[0:3], d2s)
    for ahead in range(4):
        @pl.when(z + ahead < 4)
        def _(ahead=ahead):
            sent = top_cols.at[0, 0 : ahead + 1] if ahead else top_cols.at[0, 0, 0:112]
            landed(sent, d3s.at[ahead])
    for owner, column, low, high in SOURCES:
        @pl.when((sub == owner) & (z == column))
        def _(low=low, high=high):
            landed(acc.at[0, 0, 0 : high - low, 0:112], sc_s)
    for column in range(3):
        @pl.when((z == column) & (y == 0))
        def _(column=column):
            for t in range(1, 4):
                fw_copy(t, column).wait_send()

    link_copy.wait_send()
    for n in range(subs):
        s0_copy(n).wait_send()
    for kind in range(6):
        for h in range(2):
            s1_copy(kind, h).wait_send()
    for h in range(2):
        for d in range(1, 4):
            s2_copy(h, d).wait_send()
    for d in range(1, 4):
        @pl.when(z + d < 4)
        def _():
            z_copy(d).wait_send()


def panel_solve(pattern, link, coupling, inverse, interface):
    subs, cells, faces = coupling.shape[:3]
    blocks = lambda *lead: pltpu.VMEM((*lead, BLK, BLK), F32)
    dma = lambda n: pltpu.SemaphoreType.DMA((n,))
    one = pltpu.SemaphoreType.DMA
    groups = subs * cells // GROUP
    halves_of = interface.reshape(2, BLK, BLK)
    return pl.pallas_call(
        functools.partial(panel_kernel, 4),
        out_shape=jax.ShapeDtypeStruct(interface.shape, F32),
        in_specs=[pl.BlockSpec(memory_space=pltpu.HBM)] * 5,
        out_specs=pl.BlockSpec(memory_space=pltpu.VMEM),
        scratch_shapes=[
            pltpu.SMEM(pattern.shape, jnp.int32),
            pltpu.SMEM(link.shape, jnp.int32),
            pltpu.SMEM(link.shape, jnp.int32),
            blocks(2),
            blocks(subs * cells),
            blocks(subs * cells, faces - 1),
            blocks(subs * cells),
            pltpu.VMEM((subs * cells, BLK, 2 * BLK), BF16),
            blocks(subs * (faces - 1) + 1),
            blocks(subs * (faces - 1) + 1),
            dma(3), dma(groups), dma(groups), dma(groups),
            blocks(),
            pltpu.VMEM((8, 16, BLK), F32),
            pltpu.VMEM((4, 16, BLK), F32),
            pltpu.VMEM((4, 16, BLK), F32),
            blocks(4, 4),
            blocks(4, 2, 4), blocks(2, 2), blocks(2, 2), blocks(2, 2), blocks(2, 2), blocks(2, 2), blocks(2, 2),
            blocks(6),
            pltpu.VMEM((4, 2 * BLK, BLK), F32),
            pltpu.VMEM((BLK, 2 * BLK), F32),
            blocks(6), blocks(16), blocks(4), blocks(),
            one, one, one, one, dma(4), dma(4), one, one, dma(4),
            dma(3), dma(3), dma(12), dma(12), dma(6), dma(6), dma(4), dma(4),
        ],
        compiler_params=pltpu.CompilerParams(
            collective_id=0, has_side_effects=True, vmem_limit_bytes=60 << 20
        ),
        name="panel_solve",
    )(pattern, link, coupling, inverse, halves_of)


def shards(coupling_blocks, block_inverse, coupling_pattern, link_blocks, interface_panel):
    pattern = coupling_pattern.transpose(2, 0, 1)
    return panel_solve(pattern, link_blocks, coupling_blocks, block_inverse, interface_panel)


def solution(mesh):
    in_specs = (
        P(("sub", "blk"), None, None, None, None),
        P(("sub", "blk"), None, None, None),
        P(("sub", "blk"), None, None),
        P(("sub", "blk"), None),
        P("sub", "blk"),
    )
    out_specs = P("sub", "blk")
    return jax.shard_map(shards, mesh=mesh, in_specs=in_specs, out_specs=out_specs, check_vma=False)
```

```python
import functools

import jax
import jax.numpy as jnp
from jax import lax
from jax.experimental import pallas as pl
from jax.experimental.pallas import tpu as pltpu
from jax.sharding import PartitionSpec as P

F32 = jnp.float32
BF16 = jnp.bfloat16
MESH = pl.DeviceIdType.MESH
BLK = 128
GROUP = 8
STEP = 16
HALF = BLK // 2


def halves(value):
    high = value.astype(BF16)
    return high, (value - high.astype(F32)).astype(BF16)


def product_nt(a, b):
    ah, al = halves(a)
    bh, bl = halves(b)
    return lax.dot_general(
        jnp.concatenate([ah, al, ah], axis=1),
        jnp.concatenate([bh, bh, bl], axis=1),
        (((1,), (1,)), ((), ())),
        preferred_element_type=F32,
    )


def product_nn(a, b):
    ah, al = halves(a)
    bh, bl = halves(b)
    return jnp.dot(
        jnp.concatenate([ah, al, ah], axis=1),
        jnp.concatenate([bh, bh, bl], axis=0),
        preferred_element_type=F32,
    )


def inverse_factor(pair, between):
    rows = lax.broadcasted_iota(jnp.int32, (STEP, BLK), 0)
    for r in range(0, BLK, STEP):
        pa, pe = pair[r : r + STEP, :BLK], pair[r : r + STEP, BLK:]
        t = jnp.stack([jnp.broadcast_to(pa[:, r + j : r + j + 1], (STEP, BLK)) for j in range(STEP)])
        pivots = jnp.zeros((STEP, BLK), F32)
        for k in range(STEP):
            pivot = t[0, k : k + 1, :]
            m = jnp.where(rows > k, t[0] * (1.0 / pivot), 0.0)
            pivots = jnp.where(rows == k, pivot, pivots)
            if k + 1 < STEP:
                t = t[1:] - m[None] * t[1:, k : k + 1, :]
            pa = pa - m * pa[k : k + 1]
            pe = pe - m * pe[k : k + 1]
        scale = lax.rsqrt(pivots)
        pa, pe = pa * scale, pe * scale
        pair[r : r + STEP, BLK:] = pe
        if r + STEP < BLK:
            high, low = halves(jnp.concatenate([pa, pe], axis=1))
            ah, al = high[:, :BLK], low[:, :BLK]
            change = lax.dot_general(
                jnp.concatenate([ah, ah, al], axis=0),
                jnp.concatenate([high, low, high], axis=0),
                (((0,), (0,)), ((), ())),
                preferred_element_type=F32,
            )
            pair[r + STEP :, :] = pair[r + STEP :, :] - change[r + STEP :, :]
        between(r // STEP)


def panel_kernel(
    nx, pattern_ref, link_ref, coupling_ref, inverse_ref, interface_ref, out_ref,
    pattern, link, peer_link, panel_ref, firsts, faces, inverses, rhs, links_ref, peer_links,
    small_s, inv_s, first_s, face_s,
    firstc, gather1, gather2, pieces, top_cols,
    acc, inflow, last, sall, pair, lower, inv, above, own_above, own_w, rest, top,
    d1s, d1r, d2s, d2r, d3s, d3r, of_s, of_r, sw_s, sw_r, sc_s, op_r, fw_s,
    s0s, s0r, s1s, s1a, s1b, s2s, s2r, zs, zr,
):
    sub, z = lax.axis_index("sub"), lax.axis_index("blk")
    core = lax.rem(sub, 2)
    x = lax.rem(sub // 2, nx)
    y = sub // (2 * nx)

    def sub_of(yy, xx, cc):
        return (yy * nx + xx) * 2 + cc

    def remote(src, dst, ssem, rsem, to_sub, to_z):
        return pltpu.make_async_remote_copy(
            src_ref=src, dst_ref=dst, send_sem=ssem, recv_sem=rsem,
            device_id=(to_sub, to_z), device_id_type=MESH,
        )

    q = core * 4 + x

    def row_peer(t):
        to = lax.rem(q + t, 8)
        return to, sub_of(y, lax.rem(to, 4), to // 4)

    def y_peer(t):
        return sub_of(lax.rem(y + t, 4), x, core)

    barrier = pltpu.get_barrier_semaphore()

    def greet(to_sub, to_z):
        pl.semaphore_signal(barrier, inc=1, device_id=(to_sub, to_z), device_id_type=MESH)

    for t in range(1, 8):
        greet(row_peer(t)[1], z)
    for t in range(1, 4):
        greet(y_peer(t), z)
        greet(sub, lax.rem(z + t, 4))

    subs, cells, links = coupling_ref.shape[0], coupling_ref.shape[1], coupling_ref.shape[2] - 1
    per_sub = cells // GROUP
    none = subs * links
    small = [
        pltpu.make_async_copy(pattern_ref, pattern, small_s.at[0]),
        pltpu.make_async_copy(link_ref, link, small_s.at[1]),
        pltpu.make_async_copy(interface_ref, panel_ref, small_s.at[2]),
    ]
    inv_in, first_in, face_in = [], [], []
    for g in range(subs * per_sub):
        n, c = g // per_sub, pl.ds(g % per_sub * GROUP, GROUP)
        held = pl.ds(g * GROUP, GROUP)
        inv_in.append(pltpu.make_async_copy(inverse_ref.at[n, c], inverses.at[held], inv_s.at[g]))
        first_in.append(pltpu.make_async_copy(coupling_ref.at[n, c, 0], firsts.at[held], first_s.at[g]))
        face_in.append(
            pltpu.make_async_copy(coupling_ref.at[n, c, pl.ds(1, links)], faces.at[held], face_s.at[g])
        )
    for copy in small + [copy for both in zip(inv_in, first_in) for copy in both] + face_in:
        copy.start()
    links_ref[none] = jnp.zeros((BLK, BLK), F32)
    peer_links[none] = jnp.zeros((BLK, BLK), F32)

    zero = jnp.zeros((BLK, BLK), BF16)
    small[0].wait()
    for g in range(subs * per_sub):
        inv_in[g].wait()
        first_in[g].wait()
        left, right = [], []
        for i in range(g * GROUP, g * GROUP + GROUP):
            bh, bl = halves(firsts[i] * pattern[0, i // cells, i % cells].astype(F32))
            ih, il = halves(inverses[i])
            weight = jnp.concatenate(
                [jnp.concatenate([bh, bh], axis=1), jnp.concatenate([bl, zero], axis=1)], axis=0
            )
            both = lax.dot_general(
                jnp.concatenate([ih, il], axis=1), weight, (((1,), (1,)), ((), ())),
                preferred_element_type=F32,
            )
            sh, sl = halves(both[:, :BLK] + both[:, BLK:])
            pair_hl = jnp.concatenate([sh, sl], axis=1)
            rhs[i] = pair_hl
            left += [bh, bl]
            right += [pair_hl, jnp.concatenate([sh, zero], axis=1)]
        both = jnp.dot(
            jnp.concatenate(left, axis=1), jnp.concatenate(right, axis=0), preferred_element_type=F32
        )
        part = both[:, :BLK] + both[:, BLK:]
        firstc[...] = -part if g == 0 else firstc[...] - part

    def link_updates(g):
        face_in[g].wait()
        n = g // per_sub
        highs, lows = [], []
        for i in range(g * GROUP, g * GROUP + GROUP):
            value = jnp.concatenate(
                [faces[i, l] * pattern[l + 1, n, i % cells].astype(F32) for l in range(links)], axis=0
            )
            high, low = halves(value)
            highs.append(high)
            lows.append(low)
        right = rhs[g * GROUP : (g + 1) * GROUP].reshape(GROUP * BLK, 2 * BLK)
        both = jnp.dot(jnp.concatenate(highs, axis=1), right, preferred_element_type=F32)
        rest = jnp.dot(jnp.concatenate(lows, axis=1), right[:, :BLK], preferred_element_type=F32)
        part = (both[:, :BLK] + both[:, BLK:] + rest).reshape(links, BLK, BLK)
        held = pl.ds(n * links, links)
        links_ref[held] = part if g % per_sub == 0 else links_ref[held] + part

    small[1].wait()
    small[2].wait()

    @pl.when(sub == z // 2)
    def _():
        firstc[...] += panel_ref[lax.rem(z, 2)]

    pl.semaphore_wait(barrier, 13)

    mine = pl.ds(pl.multiple_of(q * 16, 16), 16)

    def landed(ref, sem):
        pltpu.make_async_copy(ref, ref, sem).wait()

    for t in range(1, 8):
        to, to_sub = row_peer(t)
        remote(
            firstc.at[pl.ds(pl.multiple_of(to * 16, 16), 16)], gather1.at[q], d1s, d1r, to_sub, z
        ).start()
    gather1[q] = firstc[mine, :]

    SOURCES = ((0, 0, 1, 2), (1, 0, 0, 2), (1, 1, 0, 2), (1, 2, 1, 2))

    def source_copy(t, owner, low, high):
        to, to_sub = row_peer(t)
        src = panel_ref.at[low:high, pl.ds(pl.multiple_of(to * 16, 16), 16)]
        dst = pieces.at[2 * owner + low : 2 * owner + high]
        if t == 0:
            return pltpu.make_async_copy(src, dst, op_r)
        return remote(src, dst, sc_s, op_r, to_sub, z)

    for owner, column, low, high in SOURCES:
        @pl.when((sub == owner) & (z == column))
        def _(owner=owner, low=low, high=high):
            for t in range(8):
                source_copy(t, owner, low, high).start()

    peer = sub_of(y, x, 1 - core)
    link_copy = remote(link, peer_link, s0s.at[2], s0r.at[2], peer, z)
    link_copy.start()

    def s0_copy(n):
        part = pl.ds(n * links, links)
        return remote(links_ref.at[part], peer_links.at[part], s0s.at[n], s0r.at[n], peer, z)

    def fw_copy(t, column):
        part = pieces.at[column + 1 : 4]
        return remote(part, part, fw_s.at[t], op_r, y_peer(t), z)

    link_updates(0)
    link_updates(1)
    s0_copy(0).start()

    landed(gather1.at[0:7], d1r)
    gather2[y] = jnp.sum(gather1[...], axis=0)
    for t in range(1, 4):
        remote(gather2.at[y], gather2.at[y], d2s, d2r, y_peer(t), z).start()
    for column in range(3):
        @pl.when((z == column) & (y == 0))
        def _(column=column):
            landed(pieces.at[column + 1 : 4], op_r)
            for t in range(1, 4):
                fw_copy(t, column).start()

    link_updates(2)
    link_updates(3)
    s0_copy(1).start()

    landed(gather2.at[0:3], d2r)
    pieces[z] = jnp.sum(gather2[...], axis=0)
    pltpu.make_async_copy(pieces.at[z], top_cols.at[z, z, mine], d3r.at[z]).start()
    for ahead in range(3, -1, -1):
        @pl.when(z + ahead < 4)
        def _(ahead=ahead):
            def send(t, carry):
                remote(
                    pieces.at[z], top_cols.at[z, z, mine], d3s.at[ahead], d3r.at[z],
                    row_peer(t)[1], z + ahead,
                ).start()
                return carry

            lax.fori_loop(0 if ahead else 1, 8, send, 0)

    def below_send():
        for column in range(3):
            @pl.when((z == column) & (y > 0))
            def _(column=column):
                landed(pieces.at[column + 1 : 4], op_r)

        for ahead in range(3, 0, -1):
            @pl.when(z + ahead < 4)
            def _(ahead=ahead):
                part = pl.ds(z + 1, ahead)
                for xx in range(4):
                    remote(
                        pieces.at[part], top_cols.at[z, part, mine], of_s.at[ahead], of_r.at[z],
                        sub_of(y, xx, core), z + ahead,
                    ).start()

    own_half = pl.ds(pl.multiple_of(core * HALF, HALF), HALF)

    def swap_copy(j, row):
        part = top_cols.at[j, j + 1 : row + 1, own_half]
        return remote(part, part, sw_s.at[j], sw_r.at[j], peer, z)

    def each_below(act):
        for row in range(1, 4):
            @pl.when(z == row)
            def _(row=row):
                for j in range(row):
                    act(j, row)

    def below_swap():
        def act(j, row):
            landed(top_cols.at[j, j + 1 : row + 1, 0:HALF], of_r.at[j])
            swap_copy(j, row).start()

        each_below(act)

    def diagonal_arrives(j):
        @pl.when(z >= j)
        def _():
            landed(top_cols.at[j, j], d3r.at[j])

    link_copy.wait_recv()
    names = [[link[n, l] for l in range(links)] for n in range(subs)]
    peer_names = [[peer_link[n, l] for l in range(links)] for n in range(subs)]

    def slot(names, n, g):
        found = jnp.int32(none)
        for l in range(links):
            found = jnp.where(names[n][l] == g, n * links + l, found)
        return found

    def fill(r):
        def body(other, carry):
            for h in range(2):
                to_x = lax.rem(x + r, 4) if h == 0 else other
                to_y = other if h == 0 else lax.rem(y + r, 4)
                g = sub_of(to_y, to_x, core) * 2 + h
                total = links_ref[slot(names, 0, g)]
                for n in range(1, subs):
                    total = total + links_ref[slot(names, n, g)]
                for n in range(subs):
                    total = total + peer_links[slot(peer_names, n, g)]
                acc[r, h, other] = total
            return carry

        lax.fori_loop(0, 4, body, 0)

    def ring(h, step):
        if h == 0:
            return sub_of(y, lax.rem(x + step + 4, 4), core)
        return sub_of(lax.rem(y + step + 4, 4), x, core)

    def rows_of(c):
        return pl.ds(c * HALF, HALF)

    def s1_start(kinds, c):
        rows = rows_of(c)
        for kind in kinds:
            r, low, step = ((2, 0, 1), (2, 2, -1), (1, 2, 1), (3, 0, -1), (1, 0, 1), (3, 2, -1))[kind]
            for h in range(2):
                remote(
                    acc.at[r, h, low : low + 2, rows], inflow.at[kind, h, 0:2, rows],
                    s1s, (s1a if kind < 2 else s1b).at[c], ring(h, step), z,
                ).start()

    for n in range(subs):
        s0_copy(n).wait_recv()
    fill(2)
    s1_start((0, 1), 0)
    fill(1)
    fill(3)
    s1_start((2, 3), 0)
    s1_start((0, 1), 1)
    s1_start((2, 3), 1)
    below_send()
    fill(0)

    def service1(c):
        rows = rows_of(c)
        landed(inflow.at[0:2, 0:2, 0:2, rows], s1a.at[c])
        for h in range(2):
            acc[1, h, 0:2, rows] += inflow[0, h, 0:2, rows]
            acc[3, h, 2:4, rows] += inflow[1, h, 0:2, rows]
        s1_start((4, 5), c)

    def service2(c):
        rows = rows_of(c)
        landed(inflow.at[2:6, 0:2, 0:2, rows], s1b.at[c])
        for h in range(2):
            acc[0, h, 0:2, rows] += inflow[3, h, 0:2, rows] + inflow[4, h, 0:2, rows]
            acc[0, h, 2:4, rows] += inflow[2, h, 0:2, rows] + inflow[5, h, 0:2, rows]
            for d in range(1, 4):
                there = lax.rem((y if h == 0 else x) + d, 4)
                to = sub_of(there, x, core) if h == 0 else sub_of(y, there, core)
                remote(
                    acc.at[0, h, there, rows], last.at[h * 3 + d - 1, rows], s2s, s2r.at[c], to, z
                ).start()

    def z_copy(d, c, base):
        part = sall.at[base, 0:2, rows_of(c)]
        return remote(part, part, zs, zr.at[d], sub, base + d)

    def service3(c):
        rows = rows_of(c)
        landed(last.at[0:6, rows], s2r.at[c])
        for h in range(2):
            total = acc[0, h, y if h == 0 else x, rows]
            for d in range(1, 4):
                total = total + last[h * 3 + d - 1, rows]
            sall[z, h, rows] = jnp.where(sub * 2 + h == z, top[rows], panel_ref[h, rows] - total)

        for d in range(3, 0, -1):
            @pl.when(z + d < 4)
            def _():
                z_copy(d, c, z).start()

    def earlier_columns():
        rest[...] = sall[z].reshape(2 * BLK, BLK)
        for d in range(1, 4):
            @pl.when(z >= d)
            def _():
                landed(sall.at[z - d], zr.at[d])
                column = pl.ds(pl.multiple_of((z - d) * BLK, BLK), BLK)
                rest[...] -= product_nt(sall[z - d].reshape(2 * BLK, BLK), own_above[:, column])

    diagonal_arrives(0)
    unit = jnp.where(
        lax.broadcasted_iota(jnp.int32, (BLK, BLK), 0) == lax.broadcasted_iota(jnp.int32, (BLK, BLK), 1),
        1.0, 0.0,
    )
    inv[...] = jnp.zeros_like(inv)
    hooks = {
        (0, 3): lambda: service1(0),
        (0, 6): below_swap,
        (0, 7): lambda: service1(1),
        (1, 3): lambda: service2(0),
        (1, 7): lambda: service2(1),
        (2, 4): lambda: service3(0),
        (3, 0): lambda: service3(1),
        (3, 7): earlier_columns,
    }

    def row_of_inverse(k):
        if k:
            width = slice(0, k * BLK)
            inv[k * BLK : (k + 1) * BLK, width] = -product_nn(
                inv[k * BLK : (k + 1) * BLK, k * BLK : (k + 1) * BLK], above[:, width]
            )

    def subtract(k, j):
        left = lower[j:4, :, k * BLK : (k + 1) * BLK].reshape((4 - j) * BLK, BLK)
        change = product_nt(left, lower[j, :, k * BLK : (k + 1) * BLK])
        top_cols[j, j:4] = top_cols[j, j:4] - change.reshape(4 - j, BLK, BLK)

    def between(k, r):
        if k and r == 0:
            for j in range(k + 1, 4):
                subtract(k - 1, j)
            row_of_inverse(k - 1)
        if k and r == 2:
            width = slice(0, k * BLK)
            above[:, width] = product_nn(lower[k, :, width], inv[width, width])

            @pl.when(z == k)
            def _():
                own_above[...] = above[...]
        if (k, r) in hooks:
            hooks[k, r]()

    for k in range(4):
        pair[:, :BLK] = top_cols[k, k]
        pair[:, BLK:] = unit
        inverse_factor(pair, functools.partial(between, k))
        w = pair[:, BLK:]

        @pl.when(z == k)
        def _():
            own_w[...] = w

        inv[k * BLK : (k + 1) * BLK, k * BLK : (k + 1) * BLK] = w
        if k == 0:
            for j in range(1, 4):
                diagonal_arrives(j)
            each_below(lambda j, row: swap_copy(j, row).wait())
            top[...] = top_cols[z, z]
        if k < 3:
            stack = top_cols[k, k + 1 : 4].reshape((3 - k) * BLK, BLK)
            lower[k + 1 : 4, :, k * BLK : (k + 1) * BLK] = product_nt(stack, w).reshape(3 - k, BLK, BLK)
            subtract(k, k + 1)

    out_ref[...] = product_nt(rest[...], own_w[...]).reshape(2, BLK, BLK)

    landed(gather1.at[0:7], d1s)
    landed(gather2.at[0:3], d2s)
    for ahead in range(4):
        @pl.when(z + ahead < 4)
        def _(ahead=ahead):
            sent = top_cols.at[0, 0] if ahead else top_cols.at[0, 0, 0:112]
            landed(sent, d3s.at[ahead])
            if ahead:
                landed(top_cols.at[0, 0:ahead, 0:HALF], of_s.at[ahead])
    for owner, column, low, high in SOURCES:
        @pl.when((sub == owner) & (z == column))
        def _(low=low, high=high):
            landed(acc.at[0, 0, 0 : high - low, 0:112], sc_s)
    for column in range(3):
        @pl.when((z == column) & (y == 0))
        def _(column=column):
            for t in range(1, 4):
                fw_copy(t, column).wait_send()

    link_copy.wait_send()
    for n in range(subs):
        s0_copy(n).wait_send()
    landed(inflow, s1s)
    landed(last, s2s)
    for row in range(3):
        @pl.when(z == row)
        def _(row=row):
            landed(sall.at[0 : 3 - row], zs)


def panel_solve(pattern, link, coupling, inverse, interface):
    subs, cells, faces = coupling.shape[:3]
    blocks = lambda *lead: pltpu.VMEM((*lead, BLK, BLK), F32)
    dma = lambda n: pltpu.SemaphoreType.DMA((n,))
    one = pltpu.SemaphoreType.DMA
    groups = subs * cells // GROUP
    halves_of = interface.reshape(2, BLK, BLK)
    return pl.pallas_call(
        functools.partial(panel_kernel, 4),
        out_shape=jax.ShapeDtypeStruct((2, BLK, BLK), F32),
        in_specs=[pl.BlockSpec(memory_space=pltpu.HBM)] * 5,
        out_specs=pl.BlockSpec(memory_space=pltpu.VMEM),
        scratch_shapes=[
            pltpu.SMEM(pattern.shape, jnp.int32),
            pltpu.SMEM(link.shape, jnp.int32),
            pltpu.SMEM(link.shape, jnp.int32),
            blocks(2),
            blocks(subs * cells),
            blocks(subs * cells, faces - 1),
            blocks(subs * cells),
            pltpu.VMEM((subs * cells, BLK, 2 * BLK), BF16),
            blocks(subs * (faces - 1) + 1),
            blocks(subs * (faces - 1) + 1),
            dma(3), dma(groups), dma(groups), dma(groups),
            blocks(),
            pltpu.VMEM((8, 16, BLK), F32),
            pltpu.VMEM((4, 16, BLK), F32),
            pltpu.VMEM((4, 16, BLK), F32),
            blocks(4, 4),
            blocks(4, 2, 4), blocks(6, 2, 2),
            blocks(6),
            blocks(4, 2),
            pltpu.VMEM((BLK, 2 * BLK), F32),
            pltpu.VMEM((4, BLK, 4 * BLK), F32),
            pltpu.VMEM((4 * BLK, 4 * BLK), F32),
            pltpu.VMEM((BLK, 4 * BLK), F32),
            pltpu.VMEM((BLK, 4 * BLK), F32),
            blocks(),
            pltpu.VMEM((2 * BLK, BLK), F32),
            blocks(),
            one, one, one, one, dma(4), dma(4), dma(4), dma(4), dma(4), dma(4), one, one, dma(4),
            dma(3), dma(3), one, dma(2), dma(2), one, dma(2), one, dma(4),
        ],
        compiler_params=pltpu.CompilerParams(
            collective_id=0, has_side_effects=True, vmem_limit_bytes=60 << 20
        ),
        name="panel_solve",
    )(pattern, link, coupling, inverse, halves_of).reshape(interface.shape)


def shards(coupling_blocks, block_inverse, coupling_pattern, link_blocks, interface_panel):
    pattern = coupling_pattern.transpose(2, 0, 1)
    return panel_solve(pattern, link_blocks, coupling_blocks, block_inverse, interface_panel)


def solution(mesh):
    in_specs = (
        P(("sub", "blk"), None, None, None, None),
        P(("sub", "blk"), None, None, None),
        P(("sub", "blk"), None, None),
        P(("sub", "blk"), None),
        P("sub", "blk"),
    )
    out_specs = P("sub", "blk")
    return jax.shard_map(shards, mesh=mesh, in_specs=in_specs, out_specs=out_specs, check_vma=False)
```
